128 devices in a mesh: row: 16 (over y, x_hi, core), col: 8 (over z, x_lo).
Axes of the slice: x: 4 (x_hi: 2, x_lo: 2; x = x_hi * 2 + x_lo), y: 4, z: 4, core: 2. Of those that a mesh axis runs over, the one named last changes fastest.
Arguments:
- ks_matrix: float32 [6144, 6144], P('row', 'col'), as said below
- occupancy: int32 [48, 48], P('row', 'col'), may hold values from 0 to 1, as said below
Outputs:
- sign_estimate: float32 [6144, 6144], P('row', 'col')
The draws below stay inside these ranges and needn't reach their ends.
Inputs may be any that keep to these rules, and one draw needn't show every extreme that they name: `occupancy`: symmetric; every block pair at most 2 blocks from the diagonal is kept. `ks_matrix`: symmetric, and zero outside the kept block pairs.
All inputs are finite; a program needn't handle non-finite values.
Results may differ from the reference program's by a relative error of at most 0.0045.
Values may be sent and summed in bfloat16 or wider, within the bound.
No kernel may reach another device: no remote copies, remote signals or barrier semaphores. Data moves between devices by JAX's collectives and lax.ppermute only.
A program may use at most 64 MiB of HBM per device.

```python
import jax
import jax.numpy as jnp

BS = 128
STEPS = 2
NB = 48
ORDER = 6144


def occupancy_pattern(key):
    key = jax.random.fold_in(key, 11)
    tickets = jax.random.randint(key, (NB, NB), 0, 1000)
    places = jnp.arange(NB)
    distance = jnp.abs(places[:, None] - places[None, :])
    limit = jnp.maximum(80, 1000 - 120 * distance)
    upper = (tickets < limit).astype(jnp.int32)
    mirrored = jnp.where(places[:, None] <= places[None, :], upper, upper.T)
    return jnp.where(distance <= 2, 1, mirrored).astype(jnp.int32)


def draw_occupancy(key, part):
    return occupancy_pattern(key)


def draw_ks_matrix(key, part):
    pattern = occupancy_pattern(key)
    key = jax.random.fold_in(key, 5)
    first_key, second_key, third_key = jax.random.split(key, 3)
    raw = jax.random.normal(first_key, (ORDER, ORDER), jnp.float32)
    kept_share = jnp.sum(pattern).astype(jnp.float32) / (NB * NB)
    coupling = (raw + raw.T) * (0.41 / jnp.sqrt(kept_share * ORDER))
    occupied = jnp.repeat(jnp.repeat(pattern.astype(jnp.float32), BS, axis=0), BS, axis=1)
    magnitude = jax.random.uniform(second_key, (ORDER,), jnp.float32, 0.1, 0.45)
    signs = jnp.where(jax.random.randint(third_key, (ORDER,), 0, 2) == 1, 1.0, -1.0).astype(jnp.float32)
    return (occupied * coupling + jnp.diag(magnitude * signs)).astype(jnp.float32)


def setup_inputs(seed: int = 0) -> dict:
    streams_of = jax.random.split(jax.random.key(seed), 3)
    ks_matrix = draw_ks_matrix(jax.random.fold_in(streams_of[2], 71), 0)
    occupancy = draw_occupancy(jax.random.fold_in(streams_of[2], 71), 0)
    return dict(ks_matrix=ks_matrix, occupancy=occupancy)


def reference(ks_matrix, occupancy):
    occupied = jnp.repeat(jnp.repeat(occupancy.astype(jnp.float32), BS, axis=0), BS, axis=1)
    iterate = ks_matrix
    for newton_step in range(STEPS):
        iterate_half = iterate.astype(jnp.bfloat16)
        square = jnp.dot(iterate_half, iterate_half, preferred_element_type=jnp.float32)
        square_half = square.astype(jnp.bfloat16)
        cube_term = jnp.dot(iterate_half, square_half, preferred_element_type=jnp.float32)
        iterate = occupied * (1.5 * iterate - 0.5 * cube_term)
    return iterate
```

```python
import functools
import itertools

import jax
import jax.numpy as jnp
from jax import lax
from jax.experimental import pallas as pl
from jax.experimental.pallas import tpu as pltpu
from jax.sharding import PartitionSpec as P

STEPS = 2
DIMS = (("y", 4), ("xh", 2), ("core", 2), ("z", 4), ("xl", 2))


def pairs(move):
    sizes = [n for _, n in DIMS]
    names = [name for name, _ in DIMS]

    def flat(place):
        index = 0
        for name, n in DIMS:
            index = index * n + place[name] % n
        return index

    out = []
    for coords in itertools.product(*map(range, sizes)):
        place = dict(zip(names, coords))
        out.append((flat(place), flat({**place, **move(place)})))
    return out


UP = {axis: pairs(lambda p, a=axis: {a: p[a] + 1}) for axis in ("y", "z")}
DOWN = {axis: pairs(lambda p, a=axis: {a: p[a] - 1}) for axis in ("y", "z")}
INNER = pairs(lambda p: {"xl": 1 - p["xl"]})
OUTER = pairs(lambda p: {"xh": 1 - p["xh"], "xl": 1 - p["xl"]})
CORE = pairs(lambda p: {"core": 1 - p["core"]})


def send(value, perm):
    return lax.ppermute(value, ("row", "col"), perm)


def ring(own, partner, axis):
    got = {(0, 0): own, (0, 1): partner}
    got[3, 0] = send(own, UP[axis])
    got[1, 0] = send(own, DOWN[axis])
    got[2, 0] = send(got[3, 0], UP[axis])
    got[1, 1] = send(partner, DOWN[axis])
    got[3, 1] = send(partner, UP[axis])
    got[2, 1] = send(got[1, 1], DOWN[axis])
    return got


ORDER = [(0, 0), (3, 0), (1, 0), (0, 1), (2, 0), (1, 1), (3, 1), (2, 1)]


def product_kernel(last, where, *refs):
    left, mine, other = refs[:8], refs[8:16], refs[16:24]
    refs = refs[24:]
    if last:
        old, occupancy, new, new_half = refs[:4]
        refs = refs[4:]
    else:
        square_half = refs[0]
        refs = refs[1:]
    left_buf, right_buf, total, left_sem, right_sem = refs[:5]
    shift, flip, core = where[0], where[1], where[2]
    rows, cols = total.shape
    lines = mine[0].shape[0]
    for n, (offset, pair) in enumerate(ORDER):
        pltpu.make_async_copy(left[n], left_buf.at[n], left_sem.at[n]).start()
        slot = 2 * lax.rem(offset - shift + 4, 4) + lax.rem(pair + flip, 2)
        for ref, half in ((mine[n], core), (other[n], 1 - core)):
            start = pl.multiple_of(half * lines, lines)
            pltpu.make_async_copy(
                ref, right_buf.at[slot, pl.ds(start, lines)], right_sem.at[slot]
            ).start()
    if last:
        old_buf, old_sem = refs[5:7]
        old_copy = pltpu.make_async_copy(old, old_buf, old_sem)
        old_copy.start()
    width = 256
    for n, (offset, pair) in enumerate(ORDER):
        slot = 2 * offset + pair
        pltpu.make_async_copy(left[n], left_buf.at[n], left_sem.at[n]).wait()
        pltpu.make_async_copy(
            right_buf.at[slot], right_buf.at[slot], right_sem.at[slot]
        ).wait()

        @pl.loop(0, cols // width)
        def _(j, n=n, slot=slot):
            where_j = pl.ds(pl.multiple_of(j * width, width), width)
            part = jnp.dot(
                left_buf[n], right_buf[slot, :, where_j], preferred_element_type=jnp.float32
            )
            if n == 0:
                total[:, where_j] = part
            else:
                total[:, where_j] += part

    if last:
        old_copy.wait()
        up, across = occupancy.shape
        block = rows // up
        for i in range(up):
            for j in range(across):
                at = (pl.ds(i * block, block), pl.ds(j * block, block))
                kept = occupancy[i, j].astype(jnp.float32)
                value = kept * (1.5 * old_buf[at] - 0.5 * total[at])
                new[at] = value
                new_half[at] = value.astype(jnp.bfloat16)
    else:
        square_half[...] = total[...].astype(jnp.bfloat16)


def product(where, left, mine, other, old=None, occupancy=None):
    last = old is not None
    rows, cols = left[0, 0].shape
    anywhere = pl.BlockSpec(memory_space=pl.ANY)
    vmem = pl.BlockSpec(memory_space=pltpu.VMEM)
    smem = pl.BlockSpec(memory_space=pltpu.SMEM)
    half = jax.ShapeDtypeStruct((rows, cols), jnp.bfloat16)
    scratch = [
        pltpu.VMEM((8, rows, cols), jnp.bfloat16),
        pltpu.VMEM((8, 2 * rows, cols), jnp.bfloat16),
        pltpu.VMEM((rows, cols), jnp.float32),
        pltpu.SemaphoreType.DMA((8,)),
        pltpu.SemaphoreType.DMA((8,)),
    ]
    operands = [where] + [b[at] for b in (left, mine, other) for at in ORDER]
    specs = [smem] + [anywhere] * 24
    shape, out_specs = half, vmem
    if last:
        operands += [old, occupancy]
        specs += [anywhere, smem]
        shape = (jax.ShapeDtypeStruct((rows, cols), jnp.float32), half)
        out_specs = (vmem, vmem)
        scratch += [pltpu.VMEM((rows, cols), jnp.float32), pltpu.SemaphoreType.DMA]
    return pl.pallas_call(
        functools.partial(product_kernel, last),
        out_shape=shape,
        in_specs=specs,
        out_specs=out_specs,
        scratch_shapes=scratch,
        compiler_params=pltpu.CompilerParams(vmem_limit_bytes=40 * 2**20),
        cost_estimate=pl.CostEstimate(
            flops=2 * rows * cols * 16 * rows,
            bytes_accessed=2 * 24 * rows * cols,
            transcendentals=0,
        ),
    )(*operands)


def body(ks_matrix, occupancy):
    row, col = lax.axis_index("row"), lax.axis_index("col")
    where = jnp.stack(
        [
            lax.rem(col // 2 - row // 4 + 4, 4),
            lax.rem(col + row // 2, 2),
            lax.rem(row, 2),
        ]
    ).astype(jnp.int32)
    iterate = ks_matrix
    half = iterate.astype(jnp.bfloat16)
    for _ in range(STEPS):
        beside = send(half, INNER)
        across = send(beside, OUTER)
        left = ring(half, beside, "z")
        mine = ring(half, across, "y")
        other = {at: send(block, CORE) for at, block in mine.items()}
        square_half = product(where, left, mine, other)
        left = ring(square_half, send(square_half, INNER), "z")
        iterate, half = product(where, left, mine, other, iterate, occupancy)
    return iterate


def solution(mesh):
    return jax.shard_map(
        body,
        mesh=mesh,
        in_specs=(P("row", "col"), P("row", "col")),
        out_specs=P("row", "col"),
        check_vma=False,
    )
```

```python
import functools
import itertools

import jax
import jax.numpy as jnp
from jax import lax
from jax.experimental import pallas as pl
from jax.experimental.pallas import tpu as pltpu
from jax.sharding import PartitionSpec as P

STEPS = 2
DIMS = (("y", 4), ("xh", 2), ("core", 2), ("z", 4), ("xl", 2))
OWN, BESIDE = (0, 0), (0, 1)
SLOTS = [(offset, pair) for offset in range(4) for pair in range(2)]


def pairs(move):
    sizes = [n for _, n in DIMS]
    names = [name for name, _ in DIMS]

    def flat(place):
        index = 0
        for name, n in DIMS:
            index = index * n + place[name] % n
        return index

    out = []
    for coords in itertools.product(*map(range, sizes)):
        place = dict(zip(names, coords))
        out.append((flat(place), flat({**place, **move(place)})))
    return out


Y_UP = pairs(lambda p: {"y": p["y"] + 1})
Y_DOWN = pairs(lambda p: {"y": p["y"] - 1})
Z_UP = pairs(lambda p: {"z": p["z"] + 1})
Z_DOWN = pairs(lambda p: {"z": p["z"] - 1})
INNER = pairs(lambda p: {"xl": 1 - p["xl"]})
OUTER = pairs(lambda p: {"xh": 1 - p["xh"], "xl": 1 - p["xl"]})
CORE = pairs(lambda p: {"core": 1 - p["core"]})

ANYWHERE = pl.BlockSpec(memory_space=pl.ANY)
VMEM = pl.BlockSpec(memory_space=pltpu.VMEM)
SMEM = pl.BlockSpec(memory_space=pltpu.SMEM)


def send(value, perm):
    return lax.ppermute(value, ("row", "col"), perm)


def settle(**values):
    names = sorted(values)
    return dict(zip(names, lax.optimization_barrier(tuple(values[n] for n in names))))


def call(kernel, operands, specs, shapes, out_specs, scratch, pieces, aliases=None):
    return pl.pallas_call(
        kernel,
        out_shape=shapes,
        in_specs=specs,
        out_specs=out_specs,
        scratch_shapes=scratch,
        input_output_aliases=aliases or {},
        compiler_params=pltpu.CompilerParams(vmem_limit_bytes=28 * 2**20),
        cost_estimate=pl.CostEstimate(
            flops=2 * 384 * 768 * 768 * pieces,
            bytes_accessed=3 * 2 * 384 * 768 * pieces,
            transcendentals=0,
        ),
    )(*operands)


def slot_of(where, at):
    offset, pair = at
    return 2 * lax.rem(offset - where[0] + 4, 4) + lax.rem(pair + where[1], 2)


def times(left, mine, other):
    right = jnp.concatenate([mine[...], other[...]], axis=0)
    return jnp.dot(left, right, preferred_element_type=jnp.float32)


def keep(where, at, mine, other, sorted_right, sem):
    core, lines = where[2], mine.shape[0]
    copies = []
    for n, (ref, half) in enumerate(((mine, core), (other, 1 - core))):
        start = pl.multiple_of(half * lines, lines)
        copy = pltpu.make_async_copy(
            ref, sorted_right.at[slot_of(where, at), pl.ds(start, lines)], sem.at[n]
        )
        copy.start()
        copies.append(copy)
    return copies


def first_kernel(ats, later, where, *refs):
    n = len(ats)
    left, refs = refs[:8], refs[8:]
    mine, other, refs = refs[:n], refs[n : 2 * n], refs[2 * n :]
    total, picked, sorted_right, left_all, left_sem, keep_sem, pick_sem = refs
    core = where[2]
    half = left[0].shape[1] // 2
    copies = []
    for k in range(8):
        for part, source in enumerate((core, 1 - core)):
            start = pl.multiple_of(source * half, half)
            copy = pltpu.make_async_copy(
                left[k].at[:, pl.ds(start, half)],
                left_all.at[k, :, pl.ds(part * half, half)],
                left_sem.at[k, part],
            )
            copy.start()
            copies.append(copy)
    kept = []
    for k, at in enumerate(ats):
        kept += keep(where, at, mine[k], other[k], sorted_right, keep_sem.at[k])
    for copy in copies:
        copy.wait()
    picks = []
    for k, at in enumerate(later):
        copy = pltpu.make_async_copy(left_all.at[slot_of(where, at)], picked.at[k], pick_sem.at[k])
        copy.start()
        picks.append(copy)
    for k, at in enumerate(ats):
        part = times(left_all[slot_of(where, at)], mine[k], other[k])
        if k == 0:
            total[...] = part
        else:
            total[...] += part
    for copy in kept + picks:
        copy.wait()


def first(where, left, mine, other, ats, later):
    rows, cols = left[OWN].shape
    n = len(ats)
    return call(
        functools.partial(first_kernel, ats, later),
        [where] + [left[at] for at in SLOTS] + [mine[at] for at in ats] + [other[at] for at in ats],
        [SMEM] + [ANYWHERE] * 8 + [VMEM] * (2 * n),
        (
            jax.ShapeDtypeStruct((rows, cols), jnp.float32),
            jax.ShapeDtypeStruct((len(later), rows, cols), jnp.bfloat16),
            jax.ShapeDtypeStruct((8, 2 * rows, cols), jnp.bfloat16),
        ),
        (VMEM, VMEM, ANYWHERE),
        [
            pltpu.VMEM((8, rows, cols), jnp.bfloat16),
            pltpu.SemaphoreType.DMA((8, 2)),
            pltpu.SemaphoreType.DMA((n, 2)),
            pltpu.SemaphoreType.DMA((len(later),)),
        ],
        n,
    )


def second_kernel(ats, where, old_total, picked, *refs):
    n = len(ats)
    mine, other, refs = refs[:n], refs[n : 2 * n], refs[2 * n :]
    _, total, sorted_right, keep_sem = refs
    kept = []
    for k, at in enumerate(ats):
        kept += keep(where, at, mine[k], other[k], sorted_right, keep_sem.at[k])
    for k in range(n):
        part = times(picked[k], mine[k], other[k])
        total[...] = (old_total if k == 0 else total)[...] + part
    for copy in kept:
        copy.wait()


def second(where, total, picked, mine, other, sorted_right, ats):
    n = len(ats)
    return call(
        functools.partial(second_kernel, ats),
        [where, total, picked] + [mine[at] for at in ats] + [other[at] for at in ats] + [sorted_right],
        [SMEM, VMEM, VMEM] + [VMEM] * (2 * n) + [ANYWHERE],
        (
            jax.ShapeDtypeStruct(total.shape, total.dtype),
            jax.ShapeDtypeStruct(sorted_right.shape, sorted_right.dtype),
        ),
        (VMEM, ANYWHERE),
        [pltpu.SemaphoreType.DMA((n, 2))],
        n,
        {3 + 2 * n: 1},
    )


def third_kernel(at, where, total, picked, *refs):
    mine, other, _, square_half, sorted_right, keep_sem = refs[:2], refs[2:4], *refs[4:]
    core = where[2]
    lines = mine[0].shape[0]
    kept = []
    for h in range(2):
        for n, (ref, half) in enumerate(((mine[h], core), (other[h], 1 - core))):
            start = pl.multiple_of(half * 2 * lines + h * lines, lines)
            copy = pltpu.make_async_copy(
                ref, sorted_right.at[slot_of(where, at), pl.ds(start, lines)], keep_sem.at[h, n]
            )
            copy.start()
            kept.append(copy)
    right = jnp.concatenate([ref[...] for ref in (*mine, *other)], axis=0)
    last = picked.shape[0] - 1
    part = jnp.dot(picked[last], right, preferred_element_type=jnp.float32)
    square_half[...] = (total[...] + part).astype(jnp.bfloat16)
    for copy in kept:
        copy.wait()


def third(where, total, picked, mine, other, sorted_right, at):
    return call(
        functools.partial(third_kernel, at),
        [where, total, picked, *mine, *other, sorted_right],
        [SMEM, VMEM, VMEM] + [VMEM] * 4 + [ANYWHERE],
        (
            jax.ShapeDtypeStruct(total.shape, jnp.bfloat16),
            jax.ShapeDtypeStruct(sorted_right.shape, sorted_right.dtype),
        ),
        (VMEM, ANYWHERE),
        [pltpu.SemaphoreType.DMA((2, 2))],
        1,
        {7: 1},
    )


def cube_kernel(ats, has_total, *refs):
    n = len(ats)
    sorted_right, refs = refs[0], refs[1:]
    if has_total:
        old_total, refs = refs[0], refs[1:]
    left, refs = refs[:n], refs[n:]
    total, right, sem = refs
    copies = []
    for k, at in enumerate(ats):
        copy = pltpu.make_async_copy(sorted_right.at[SLOTS.index(at)], right.at[k], sem.at[k])
        copy.start()
        copies.append(copy)
    for k in range(n):
        copies[k].wait()
        part = jnp.dot(left[k][...], right[k], preferred_element_type=jnp.float32)
        if k == 0 and not has_total:
            total[...] = part
        else:
            total[...] = (old_total if k == 0 else total)[...] + part


def cube(sorted_right, total, left, ats):
    n = len(ats)
    rows, cols = left[OWN].shape
    has_total = total is not None
    return call(
        functools.partial(cube_kernel, ats, has_total),
        [sorted_right] + ([total] if has_total else []) + [left[at] for at in ats],
        [ANYWHERE] + [VMEM] * (n + has_total),
        jax.ShapeDtypeStruct((rows, cols), jnp.float32),
        VMEM,
        [pltpu.VMEM((n, 2 * rows, cols), jnp.bfloat16), pltpu.SemaphoreType.DMA((n,))],
        n,
    )


def final_kernel(at, occupancy, sorted_right, total, old, *refs):
    thirds, (new, new_half, right, sem) = refs[:3], refs[3:]
    copy = pltpu.make_async_copy(sorted_right.at[SLOTS.index(at)], right, sem)
    copy.start()
    rows, cols = total.shape
    up, across = occupancy.shape
    block = rows // up
    copy.wait()
    left = jnp.concatenate([ref[...] for ref in thirds], axis=0)
    new[...] = total[...] + jnp.dot(left, right[...], preferred_element_type=jnp.float32)
    for i in range(up):
        for j in range(across):
            here = (pl.ds(i * block, block), pl.ds(j * block, block))
            kept = occupancy[i, j].astype(jnp.float32)
            value = kept * (1.5 * old[here] - 0.5 * new[here])
            new[here] = value
            new_half[here] = value.astype(jnp.bfloat16)


def final(occupancy, sorted_right, total, old, thirds, at):
    rows, cols = total.shape
    return call(
        functools.partial(final_kernel, at),
        [occupancy, sorted_right, total, old, *thirds],
        [SMEM, ANYWHERE, VMEM, VMEM] + [VMEM] * 3,
        (
            jax.ShapeDtypeStruct((rows, cols), jnp.float32),
            jax.ShapeDtypeStruct((rows, cols), jnp.bfloat16),
        ),
        (VMEM, VMEM),
        [pltpu.VMEM((2 * rows, cols), jnp.bfloat16), pltpu.SemaphoreType.DMA],
        1,
    )


def newton_step(where, iterate, half, occupancy):
    middle = half.shape[0] // 2
    z, y, o = {OWN: half}, {OWN: half}, {}
    s = settle(
        beside=send(half, INNER),
        z30=send(half, Z_UP),
        z10=send(half, Z_DOWN),
        y30=send(half, Y_UP),
        y10=send(half, Y_DOWN),
    )
    z[BESIDE], z[3, 0], z[1, 0], y[3, 0], y[1, 0] = (
        s[k] for k in ("beside", "z30", "z10", "y30", "y10")
    )
    s = settle(
        across=send(z[BESIDE], OUTER),
        z20=send(z[3, 0], Z_UP),
        z11=send(z[BESIDE], Z_DOWN),
        y20=send(y[3, 0], Y_UP),
        o00=send(half, CORE),
        o30=send(y[3, 0], CORE),
        o10=send(y[1, 0], CORE),
        beside=z[BESIDE],
    )
    y[BESIDE], z[2, 0], z[1, 1], y[2, 0], o[OWN], o[3, 0], o[1, 0], z[BESIDE] = (
        s[k] for k in ("across", "z20", "z11", "y20", "o00", "o30", "o10", "beside")
    )
    s = settle(
        z31=send(z[BESIDE], Z_UP),
        z21=send(z[1, 1], Z_DOWN),
        y31=send(y[BESIDE], Y_UP),
        y11=send(y[BESIDE], Y_DOWN),
        o20=send(y[2, 0], CORE),
        o01=send(y[BESIDE], CORE),
    )
    z[3, 1], z[2, 1], y[3, 1], y[1, 1], o[2, 0], o[BESIDE] = (
        s[k] for k in ("z31", "z21", "y31", "y11", "o20", "o01")
    )
    upper, lower = send(y[3, 1][:middle], Y_UP), send(y[1, 1][middle:], Y_DOWN)
    o[3, 1], o[1, 1] = send(y[3, 1], CORE), send(y[1, 1], CORE)
    early = (OWN, (3, 0), (1, 0), (2, 0), BESIDE)
    late = ((3, 1), (1, 1), (2, 1))
    total, picked, sorted_right = first(where, z, y, o, early, late)
    s = settle(
        upper=upper, lower=lower, o31=o[3, 1], o11=o[1, 1],
        total=total, picked=picked, sorted_right=sorted_right,
    )
    upper, lower, o[3, 1], o[1, 1] = (s[k] for k in ("upper", "lower", "o31", "o11"))
    total, picked, sorted_right = (s[k] for k in ("total", "picked", "sorted_right"))
    other = send(upper, CORE), send(lower, CORE)
    total, sorted_right = second(where, total, picked, y, o, sorted_right, late[:2])
    square_half, sorted_right = third(
        where, total, picked, (upper, lower), other, sorted_right, late[2]
    )

    z = {OWN: square_half}
    s = settle(
        beside=send(square_half, INNER),
        z30=send(square_half, Z_UP),
        z10=send(square_half, Z_DOWN),
    )
    z[BESIDE], z[3, 0], z[1, 0] = (s[k] for k in ("beside", "z30", "z10"))
    z20, z11, z31 = send(z[3, 0], Z_UP), send(z[BESIDE], Z_DOWN), send(z[3, 0], INNER)
    total = cube(sorted_right, None, z, (OWN, (3, 0), (1, 0), BESIDE))
    s = settle(z20=z20, z11=z11, z31=z31, total=total)
    z[2, 0], z[1, 1], z[3, 1], total = (s[k] for k in ("z20", "z11", "z31", "total"))
    third_of = half.shape[0] // 3
    thirds = (
        send(z[3, 1][:third_of], Z_UP),
        send(z[1, 1][third_of : 2 * third_of], Z_DOWN),
        send(z[2, 0][2 * third_of :], INNER),
    )
    total = cube(sorted_right, total, z, ((2, 0), (1, 1), (3, 1)))
    return final(occupancy, sorted_right, total, iterate, thirds, (2, 1))


def body(ks_matrix, occupancy):
    row, col = lax.axis_index("row"), lax.axis_index("col")
    where = jnp.stack(
        [
            lax.rem(col // 2 - row // 4 + 4, 4),
            lax.rem(col + row // 2, 2),
            lax.rem(row, 2),
        ]
    ).astype(jnp.int32)
    where, iterate = lax.optimization_barrier((where, ks_matrix))
    half = iterate.astype(jnp.bfloat16)
    for _ in range(STEPS):
        iterate, half = newton_step(where, iterate, half, occupancy)
    return iterate


def solution(mesh):
    return jax.shard_map(
        body,
        mesh=mesh,
        in_specs=(P("row", "col"), P("row", "col")),
        out_specs=P("row", "col"),
        check_vma=False,
    )
```

```python
import functools
import itertools

import jax
import jax.numpy as jnp
from jax import lax
from jax.experimental import pallas as pl
from jax.experimental.pallas import tpu as pltpu
from jax.sharding import PartitionSpec as P

STEPS = 2
DIMS = (("y", 4), ("xh", 2), ("core", 2), ("z", 4), ("xl", 2))
OWN, BESIDE = (0, 0), (0, 1)
SLOTS = [(offset, pair) for offset in range(4) for pair in range(2)]
EARLY = (OWN, (3, 0), (1, 0), (2, 0), BESIDE)
LATE = ((3, 1), (1, 1), (2, 1))
LAST_LEFT = ((3, 1), (2, 1))


def pairs(move):
    sizes = [n for _, n in DIMS]
    names = [name for name, _ in DIMS]

    def flat(place):
        index = 0
        for name, n in DIMS:
            index = index * n + place[name] % n
        return index

    out = []
    for coords in itertools.product(*map(range, sizes)):
        place = dict(zip(names, coords))
        out.append((flat(place), flat({**place, **move(place)})))
    return out


Y_UP = pairs(lambda p: {"y": p["y"] + 1})
Y_DOWN = pairs(lambda p: {"y": p["y"] - 1})
Z_UP = pairs(lambda p: {"z": p["z"] + 1})
Z_DOWN = pairs(lambda p: {"z": p["z"] - 1})
INNER = pairs(lambda p: {"xl": 1 - p["xl"]})
OUTER = pairs(lambda p: {"xh": 1 - p["xh"], "xl": 1 - p["xl"]})
ACROSS = pairs(lambda p: {"xh": 1 - p["xh"]})
CORE = pairs(lambda p: {"core": 1 - p["core"]})

ANYWHERE = pl.BlockSpec(memory_space=pl.ANY)
VMEM = pl.BlockSpec(memory_space=pltpu.VMEM)
SMEM = pl.BlockSpec(memory_space=pltpu.SMEM)


def send(value, perm):
    return lax.ppermute(value, ("row", "col"), perm)


def join_send(values, perm):
    rows = values[0].shape[0]
    got = send(jnp.concatenate(values), perm)
    return [got[n * rows : (n + 1) * rows] for n in range(len(values))]


def settle(*values):
    return lax.optimization_barrier(values)


def call(kernel, operands, specs, shapes, out_specs, scratch, pieces, aliases=None):
    return pl.pallas_call(
        kernel,
        out_shape=shapes,
        in_specs=specs,
        out_specs=out_specs,
        scratch_shapes=scratch,
        input_output_aliases=aliases or {},
        compiler_params=pltpu.CompilerParams(vmem_limit_bytes=28 * 2**20),
        cost_estimate=pl.CostEstimate(
            flops=2 * 384 * 768 * 768 * pieces,
            bytes_accessed=3 * 2 * 384 * 768 * pieces,
            transcendentals=0,
        ),
    )(*operands)


def slot_of(where, at):
    offset, pair = at
    return 2 * lax.rem(offset - where[0] + 4, 4) + lax.rem(pair + where[1], 2)


def times(left, mine, other):
    right = jnp.concatenate([mine[...], other[...]], axis=0)
    return jnp.dot(left, right, preferred_element_type=jnp.float32)


def keep(where, at, mine, other, sorted_right, sem):
    core, lines = where[2], mine.shape[0]
    copies = []
    for n, (ref, half) in enumerate(((mine, core), (other, 1 - core))):
        start = pl.multiple_of(half * lines, lines)
        copy = pltpu.make_async_copy(
            ref, sorted_right.at[slot_of(where, at), pl.ds(start, lines)], sem.at[n]
        )
        copy.start()
        copies.append(copy)
    return copies


def early_kernel(again, ats, where, *refs):
    m, n = len(ats), len(EARLY)
    left, mine, other, refs = refs[:m], refs[m : m + n], refs[m + n : m + 2 * n], refs[m + 2 * n :]
    if again:
        old_total, total, picked, left_all, left_sem, pick_sem = refs
    else:
        total, sorted_right, left_all, left_sem, keep_sem = refs
    core = where[2]
    half = left[0].shape[1] // 2
    copies = []
    for k, at in enumerate(ats):
        for part, source in enumerate((core, 1 - core)):
            start = pl.multiple_of(source * half, half)
            copy = pltpu.make_async_copy(
                left[k].at[:, pl.ds(start, half)],
                left_all.at[SLOTS.index(at), :, pl.ds(part * half, half)],
                left_sem.at[k, part],
            )
            copy.start()
            copies.append(copy)
    kept = []
    if again:
        total[...] = old_total[...]
    else:
        for k, at in enumerate(EARLY):
            kept += keep(where, at, mine[k], other[k], sorted_right, keep_sem.at[k])
        total[...] = jnp.zeros_like(total)
    for copy in copies:
        copy.wait()
    if again:
        for k, at in enumerate(LATE):
            copy = pltpu.make_async_copy(
                left_all.at[slot_of(where, at)], picked.at[k], pick_sem.at[k]
            )
            copy.start()
            kept.append(copy)
    for k, at in enumerate(EARLY):
        slot = slot_of(where, at)
        lacked = functools.reduce(
            jnp.logical_or, [slot == SLOTS.index(last) for last in LAST_LEFT]
        )

        @pl.when(lacked if again else jnp.logical_not(lacked))
        def _(k=k, slot=slot):
            total[...] += times(left_all[slot], mine[k], other[k])

    for copy in kept:
        copy.wait()


def early(where, left, mine, other, total=None):
    rows, cols = left[OWN].shape
    n = len(EARLY)
    again = total is not None
    ats = [at for at in SLOTS if again or at not in LAST_LEFT]
    m = len(ats)
    product = jax.ShapeDtypeStruct((rows, cols), jnp.float32)
    if again:
        other_shape, other_spec = (len(LATE), rows, cols), VMEM
    else:
        other_shape, other_spec = (8, 2 * rows, cols), ANYWHERE
    return call(
        functools.partial(early_kernel, again, ats),
        [where]
        + [left[at] for at in ats]
        + [mine[at] for at in EARLY]
        + [other[at] for at in EARLY]
        + ([total] if again else []),
        [SMEM] + [ANYWHERE] * m + [VMEM] * (2 * n + again),
        (product, jax.ShapeDtypeStruct(other_shape, jnp.bfloat16)),
        (VMEM, other_spec),
        [
            pltpu.VMEM((8, rows, cols), jnp.bfloat16),
            pltpu.SemaphoreType.DMA((m, 2)),
            pltpu.SemaphoreType.DMA((len(LATE),) if again else (n, 2)),
        ],
        2 if again else n,
    )


def late_kernel(where, total, picked, *refs):
    n = len(LATE)
    mine, other, refs = refs[:n], refs[n : 2 * n], refs[2 * n :]
    _, square_half, sorted_right, keep_sem = refs
    kept = []
    for k, at in enumerate(LATE):
        kept += keep(where, at, mine[k], other[k], sorted_right, keep_sem.at[k])
    value = total[...]
    for k in range(n):
        value += times(picked[k], mine[k], other[k])
    square_half[...] = value.astype(jnp.bfloat16)
    for copy in kept:
        copy.wait()


def late(where, total, picked, mine, other, sorted_right):
    n = len(LATE)
    return call(
        late_kernel,
        [where, total, picked]
        + [mine[at] for at in LATE]
        + [other[at] for at in LATE]
        + [sorted_right],
        [SMEM, VMEM, VMEM] + [VMEM] * (2 * n) + [ANYWHERE],
        (
            jax.ShapeDtypeStruct(total.shape, jnp.bfloat16),
            jax.ShapeDtypeStruct(sorted_right.shape, sorted_right.dtype),
        ),
        (VMEM, ANYWHERE),
        [pltpu.SemaphoreType.DMA((n, 2))],
        n,
        {3 + 2 * n: 1},
    )


def cube_kernel(ats, has_total, *refs):
    n = len(ats)
    right, refs = refs[0], refs[1:]
    if has_total:
        old_total, refs = refs[0], refs[1:]
    left, total = refs[:n], refs[n]
    for k, at in enumerate(ats):
        part = jnp.dot(
            left[k][...], right[SLOTS.index(at)], preferred_element_type=jnp.float32
        )
        if k == 0 and not has_total:
            total[...] = part
        else:
            total[...] = (old_total if k == 0 else total)[...] + part


def cube(sorted_right, total, left, ats):
    n = len(ats)
    rows, cols = left[OWN].shape
    has_total = total is not None
    return call(
        functools.partial(cube_kernel, ats, has_total),
        [sorted_right] + ([total] if has_total else []) + [left[at] for at in ats],
        [VMEM] * (1 + n + has_total),
        jax.ShapeDtypeStruct((rows, cols), jnp.float32),
        VMEM,
        [],
        n,
    )


def final_kernel(at, occupancy, right, total, old, *refs):
    thirds, (new, new_half) = refs[:3], refs[3:]
    rows, cols = total.shape
    up, across = occupancy.shape
    block = rows // up
    left = jnp.concatenate([ref[...] for ref in thirds], axis=0)
    new[...] = total[...] + jnp.dot(
        left, right[SLOTS.index(at)], preferred_element_type=jnp.float32
    )
    for i in range(up):
        for j in range(across):
            here = (pl.ds(i * block, block), pl.ds(j * block, block))
            kept = occupancy[i, j].astype(jnp.float32)
            value = kept * (1.5 * old[here] - 0.5 * new[here])
            new[here] = value
            new_half[here] = value.astype(jnp.bfloat16)


def final(occupancy, sorted_right, total, old, thirds, at):
    rows, cols = total.shape
    return call(
        functools.partial(final_kernel, at),
        [occupancy, sorted_right, total, old, *thirds],
        [SMEM, VMEM, VMEM, VMEM] + [VMEM] * 3,
        (
            jax.ShapeDtypeStruct((rows, cols), jnp.float32),
            jax.ShapeDtypeStruct((rows, cols), jnp.bfloat16),
        ),
        (VMEM, VMEM),
        [],
        1,
    )


def newton_step(where, iterate, half, occupancy):
    middle = half.shape[0] // 2
    beside, z30, z10 = send(half, INNER), send(half, Z_UP), send(half, Z_DOWN)
    z10, z30, beside = settle(z10, z30, beside)
    y30, y10 = send(half, Y_UP), send(half, Y_DOWN)
    y10, y30, *_ = settle(y10, y30, z10, z30, beside)
    across, z11 = send(beside, OUTER), send(beside, Z_DOWN)
    z20 = send(z30, Z_UP)
    top, bottom = send(y30[:middle], Y_UP), send(y10[middle:], Y_DOWN)
    top, bottom, z11, z20, across, own = settle(top, bottom, z11, z20, across, half)
    y20 = jnp.concatenate([top, bottom])
    y31, y11, y21 = send(across, Y_UP), send(across, Y_DOWN), send(y20, ACROSS)
    z31, z21 = send(beside, Z_UP), send(z11, Z_DOWN)
    o = dict(zip(EARLY, join_send((own, y30, y10, y20, across), CORE)))
    y = {OWN: half, BESIDE: across, (3, 0): y30, (1, 0): y10, (2, 0): y20}
    z = {OWN: half, BESIDE: beside, (3, 0): z30, (1, 0): z10, (2, 0): z20, (1, 1): z11}
    total, sorted_right = early(where, z, y, o)
    total, sorted_right, y31, y11, y21, z31, z21 = settle(
        total, sorted_right, y31, y11, y21, z31, z21
    )
    z |= {(3, 1): z31, (2, 1): z21}
    y |= {(3, 1): y31, (1, 1): y11, (2, 1): y21}
    o |= dict(zip(LATE, join_send((y31, y11, y21), CORE)))
    total, picked = early(where, z, y, o, total)
    square_half, sorted_right = late(where, total, picked, y, o, sorted_right)

    z = {OWN: square_half}
    z[1, 0], z[3, 0], z[BESIDE] = settle(
        send(square_half, Z_DOWN), send(square_half, Z_UP), send(square_half, INNER)
    )
    z20, z11, z31 = send(z[3, 0], Z_UP), send(z[BESIDE], Z_DOWN), send(z[3, 0], INNER)
    total = cube(sorted_right, None, z, (OWN, (3, 0), (1, 0), BESIDE))
    z[2, 0], z[1, 1], z[3, 1], total = settle(z20, z11, z31, total)
    third_of = half.shape[0] // 3
    thirds = (
        send(z[3, 1][:third_of], Z_UP),
        send(z[1, 1][third_of : 2 * third_of], Z_DOWN),
        send(z[2, 0][2 * third_of :], INNER),
    )
    total = cube(sorted_right, total, z, ((2, 0), (1, 1), (3, 1)))
    return final(occupancy, sorted_right, total, iterate, thirds, (2, 1))


def body(ks_matrix, occupancy):
    row, col = lax.axis_index("row"), lax.axis_index("col")
    where = jnp.stack(
        [
            lax.rem(col // 2 - row // 4 + 4, 4),
            lax.rem(col + row // 2, 2),
            lax.rem(row, 2),
        ]
    ).astype(jnp.int32)
    where, iterate = lax.optimization_barrier((where, ks_matrix))
    half = iterate.astype(jnp.bfloat16)
    for _ in range(STEPS):
        iterate, half = newton_step(where, iterate, half, occupancy)
    return iterate


def solution(mesh):
    return jax.shard_map(
        body,
        mesh=mesh,
        in_specs=(P("row", "col"), P("row", "col")),
        out_specs=P("row", "col"),
        check_vma=False,
    )
```

```python
import functools
import itertools

import jax
import jax.numpy as jnp
from jax import lax
from jax.experimental import pallas as pl
from jax.experimental.pallas import tpu as pltpu
from jax.sharding import PartitionSpec as P

STEPS = 2
DIMS = (("y", 4), ("xh", 2), ("core", 2), ("z", 4), ("xl", 2))
OWN, BESIDE = (0, 0), (0, 1)
SLOTS = [(offset, pair) for offset in range(4) for pair in range(2)]
EARLY = (OWN, (3, 0), (1, 0), (2, 0), BESIDE)
LATE = ((3, 1), (1, 1), (2, 1))
LAST_LEFT = ((3, 1), (2, 1))


def pairs(move):
    sizes = [n for _, n in DIMS]
    names = [name for name, _ in DIMS]

    def flat(place):
        index = 0
        for name, n in DIMS:
            index = index * n + place[name] % n
        return index

    out = []
    for coords in itertools.product(*map(range, sizes)):
        place = dict(zip(names, coords))
        out.append((flat(place), flat({**place, **move(place)})))
    return out


Y_UP = pairs(lambda p: {"y": p["y"] + 1})
Y_DOWN = pairs(lambda p: {"y": p["y"] - 1})
Z_UP = pairs(lambda p: {"z": p["z"] + 1})
Z_DOWN = pairs(lambda p: {"z": p["z"] - 1})
INNER = pairs(lambda p: {"xl": 1 - p["xl"]})
OUTER = pairs(lambda p: {"xh": 1 - p["xh"], "xl": 1 - p["xl"]})
ACROSS = pairs(lambda p: {"xh": 1 - p["xh"]})
CORE = pairs(lambda p: {"core": 1 - p["core"]})

ANYWHERE = pl.BlockSpec(memory_space=pl.ANY)
VMEM = pl.BlockSpec(memory_space=pltpu.VMEM)
SMEM = pl.BlockSpec(memory_space=pltpu.SMEM)


def send(value, perm):
    return lax.ppermute(value, ("row", "col"), perm)


def join_send(values, perm):
    rows = values[0].shape[0]
    got = send(jnp.concatenate(values), perm)
    return [got[n * rows : (n + 1) * rows] for n in range(len(values))]


def settle(*values):
    return lax.optimization_barrier(values)


def call(kernel, operands, specs, shapes, out_specs, scratch, pieces, aliases=None):
    return pl.pallas_call(
        kernel,
        out_shape=shapes,
        in_specs=specs,
        out_specs=out_specs,
        scratch_shapes=scratch,
        input_output_aliases=aliases or {},
        compiler_params=pltpu.CompilerParams(vmem_limit_bytes=28 * 2**20),
        cost_estimate=pl.CostEstimate(
            flops=2 * 384 * 768 * 768 * pieces,
            bytes_accessed=3 * 2 * 384 * 768 * pieces,
            transcendentals=0,
        ),
    )(*operands)


def slot_of(where, at):
    offset, pair = at
    return 2 * lax.rem(offset - where[0] + 4, 4) + lax.rem(pair + where[1], 2)


def times(left, mine, other):
    right = jnp.concatenate([mine[...], other[...]], axis=0)
    return jnp.dot(left, right, preferred_element_type=jnp.float32)


def keep(where, at, mine, other, sorted_right, sem):
    core, lines = where[2], mine.shape[0]
    copies = []
    for n, (ref, half) in enumerate(((mine, core), (other, 1 - core))):
        start = pl.multiple_of(half * lines, lines)
        copy = pltpu.make_async_copy(
            ref, sorted_right.at[slot_of(where, at), pl.ds(start, lines)], sem.at[n]
        )
        copy.start()
        copies.append(copy)
    return copies


def early_kernel(again, ats, where, *refs):
    m, n = len(ats), len(EARLY)
    left, mine, other, refs = refs[:m], refs[m : m + n], refs[m + n : m + 2 * n], refs[m + 2 * n :]
    if again:
        late, refs = refs[: len(LATE)], refs[len(LATE) :]
        old_total, total, picked, left_all, left_sem, pick_sem = refs
    else:
        total, sorted_right, left_all, left_sem, keep_sem = refs
    core = where[2]
    half = left[0].shape[1] // 2
    copies = []
    for k, at in enumerate(ats):
        for part, source in enumerate((core, 1 - core)):
            start = pl.multiple_of(source * half, half)
            copy = pltpu.make_async_copy(
                left[k].at[:, pl.ds(start, half)],
                left_all.at[SLOTS.index(at), :, pl.ds(part * half, half)],
                left_sem.at[k, part],
            )
            copy.start()
            copies.append(copy)
    kept = []
    if again:
        total[...] = old_total[...]
    else:
        for k, at in enumerate(EARLY):
            kept += keep(where, at, mine[k], other[k], sorted_right, keep_sem.at[k])
        total[...] = jnp.zeros_like(total)
    for copy in copies:
        copy.wait()
    if again:
        for k, at in enumerate(LATE):
            copy = pltpu.make_async_copy(
                left_all.at[slot_of(where, at)], picked.at[k], pick_sem.at[k]
            )
            copy.start()
            kept.append(copy)
    for k, at in enumerate(EARLY):
        slot = slot_of(where, at)
        lacked = functools.reduce(
            jnp.logical_or, [slot == SLOTS.index(last) for last in LAST_LEFT]
        )

        @pl.when(lacked if again else jnp.logical_not(lacked))
        def _(k=k, slot=slot):
            total[...] += times(left_all[slot], mine[k], other[k])

    for copy in kept:
        copy.wait()
    if again:
        value = total[...]
        for k, ref in enumerate(late):
            value += jnp.dot(picked[k, :, :half], ref[...], preferred_element_type=jnp.float32)
        total[...] = value


def early(where, left, mine, other, total=None):
    rows, cols = left[OWN].shape
    n = len(EARLY)
    again = total is not None
    ats = [at for at in SLOTS if again or at not in LAST_LEFT]
    m = len(ats)
    product = jax.ShapeDtypeStruct((rows, cols), jnp.float32)
    if again:
        other_shape, other_spec = (len(LATE), rows, cols), VMEM
    else:
        other_shape, other_spec = (8, 2 * rows, cols), ANYWHERE
    return call(
        functools.partial(early_kernel, again, ats),
        [where]
        + [left[at] for at in ats]
        + [mine[at] for at in EARLY]
        + [other[at] for at in EARLY]
        + ([mine[at] for at in LATE] + [total] if again else []),
        [SMEM] + [ANYWHERE] * m + [VMEM] * (2 * n + (len(LATE) + 1) * again),
        (product, jax.ShapeDtypeStruct(other_shape, jnp.bfloat16)),
        (VMEM, other_spec),
        [
            pltpu.VMEM((8, rows, cols), jnp.bfloat16),
            pltpu.SemaphoreType.DMA((m, 2)),
            pltpu.SemaphoreType.DMA((len(LATE),) if again else (n, 2)),
        ],
        2 if again else n,
    )


def late_kernel(total, picked, *refs):
    other, square_half = refs[:-1], refs[-1]
    half = picked.shape[2] // 2
    value = total[...]
    for k, ref in enumerate(other):
        value += jnp.dot(picked[k, :, half:], ref[...], preferred_element_type=jnp.float32)
    square_half[...] = value.astype(jnp.bfloat16)


def late(total, picked, other):
    n = len(LATE)
    return call(
        late_kernel,
        [total, picked] + [other[at] for at in LATE],
        [VMEM] * (2 + n),
        jax.ShapeDtypeStruct(total.shape, jnp.bfloat16),
        VMEM,
        [],
        2,
    )


def place_kernel(where, *refs):
    n = len(LATE)
    mine, other, refs = refs[:n], refs[n : 2 * n], refs[2 * n :]
    _, sorted_right, keep_sem = refs
    kept = []
    for k, at in enumerate(LATE):
        kept += keep(where, at, mine[k], other[k], sorted_right, keep_sem.at[k])
    for copy in kept:
        copy.wait()


def place(where, mine, other, sorted_right):
    n = len(LATE)
    return call(
        place_kernel,
        [where] + [mine[at] for at in LATE] + [other[at] for at in LATE] + [sorted_right],
        [SMEM] + [ANYWHERE] * (2 * n + 1),
        jax.ShapeDtypeStruct(sorted_right.shape, sorted_right.dtype),
        ANYWHERE,
        [pltpu.SemaphoreType.DMA((n, 2))],
        2,
        {1 + 2 * n: 0},
    )


def product_kernel(ats, has_total, *refs):
    right, refs = refs[0], refs[1:]
    left, out = refs[-1 - len(ats) : -1], refs[-1]
    value = refs[0][...] if has_total else None
    for k, at in enumerate(ats):
        part = jnp.dot(
            left[k][...], right[SLOTS.index(at)], preferred_element_type=jnp.float32
        )
        value = part if value is None else value + part
    out[...] = value.astype(out.dtype)


def product(sorted_right, total, left, ats, dtype=jnp.float32):
    n = len(ats)
    has_total = total is not None
    return call(
        functools.partial(product_kernel, ats, has_total),
        [sorted_right] + ([total] if has_total else []) + [left[at] for at in ats],
        [VMEM] * (1 + n + has_total),
        jax.ShapeDtypeStruct(left[ats[0]].shape, dtype),
        VMEM,
        [],
        n,
    )


def final_kernel(at, occupancy, right, total, old, *refs):
    thirds, (new, new_half) = refs[:3], refs[3:]
    rows, cols = total.shape
    up, across = occupancy.shape
    block = rows // up
    left = jnp.concatenate([ref[...] for ref in thirds], axis=0)
    new[...] = total[...] + jnp.dot(
        left, right[SLOTS.index(at)], preferred_element_type=jnp.float32
    )
    for i in range(up):
        for j in range(across):
            here = (pl.ds(i * block, block), pl.ds(j * block, block))
            kept = occupancy[i, j].astype(jnp.float32)
            value = kept * (1.5 * old[here] - 0.5 * new[here])
            new[here] = value
            new_half[here] = value.astype(jnp.bfloat16)


def final(occupancy, sorted_right, total, old, thirds, at):
    rows, cols = total.shape
    return call(
        functools.partial(final_kernel, at),
        [occupancy, sorted_right, total, old, *thirds],
        [SMEM, VMEM, VMEM, VMEM] + [VMEM] * 3,
        (
            jax.ShapeDtypeStruct((rows, cols), jnp.float32),
            jax.ShapeDtypeStruct((rows, cols), jnp.bfloat16),
        ),
        (VMEM, VMEM),
        [],
        1,
    )


def newton_step(where, iterate, half, occupancy):
    middle = half.shape[0] // 2
    beside, z30, z10 = send(half, INNER), send(half, Z_UP), send(half, Z_DOWN)
    z10, z30, beside = settle(z10, z30, beside)
    y30, y10 = send(half, Y_UP), send(half, Y_DOWN)
    y10, y30, *_ = settle(y10, y30, z10, z30, beside)
    across, z11 = send(beside, OUTER), send(beside, Z_DOWN)
    z20 = send(z30, Z_UP)
    top, bottom = send(y30[:middle], Y_UP), send(y10[middle:], Y_DOWN)
    top, bottom, z11, z20, across, own = settle(top, bottom, z11, z20, across, half)
    y20 = jnp.concatenate([top, bottom])
    y31, y11, y21 = send(across, Y_UP), send(across, Y_DOWN), send(y20, ACROSS)
    *swapped, up, down = settle(*join_send((own, y30, y10, y20, across), CORE), beside, z11)
    z31, z21 = send(up, Z_UP), send(down, Z_DOWN)
    o = dict(zip(EARLY, swapped))
    y = {OWN: half, BESIDE: across, (3, 0): y30, (1, 0): y10, (2, 0): y20}
    z = {OWN: half, BESIDE: beside, (3, 0): z30, (1, 0): z10, (2, 0): z20, (1, 1): z11}
    total, sorted_right = early(where, z, y, o)
    total, sorted_right, y31, y11, y21, z31, z21 = settle(
        total, sorted_right, y31, y11, y21, z31, z21
    )
    z |= {(3, 1): z31, (2, 1): z21}
    y |= {(3, 1): y31, (1, 1): y11, (2, 1): y21}
    o |= dict(zip(LATE, join_send((y31, y11, y21), CORE)))
    total, picked = early(where, z, y, o, total)
    square_half = late(total, picked, o)
    square_half, sorted_right = settle(square_half, sorted_right)
    sorted_right = place(where, y, o, sorted_right)

    z = {OWN: square_half}
    z[1, 0], z[3, 0], z[BESIDE] = settle(
        send(square_half, Z_DOWN), send(square_half, Z_UP), send(square_half, INNER)
    )
    z20, z11, z31 = send(z[3, 0], Z_UP), send(z[BESIDE], Z_DOWN), send(z[3, 0], INNER)
    total = product(sorted_right, None, z, (OWN, (3, 0), (1, 0), BESIDE))
    z[2, 0], z[1, 1], z[3, 1] = z20, z11, z31
    third_of = half.shape[0] // 3
    thirds = (
        send(z[3, 1][:third_of], Z_UP),
        send(z[1, 1][third_of : 2 * third_of], Z_DOWN),
        send(z[2, 0][2 * third_of :], INNER),
    )
    total = product(sorted_right, total, z, ((2, 0), (1, 1), (3, 1)))
    return final(occupancy, sorted_right, total, iterate, thirds, (2, 1))


def body(ks_matrix, occupancy):
    row, col = lax.axis_index("row"), lax.axis_index("col")
    where = jnp.stack(
        [
            lax.rem(col // 2 - row // 4 + 4, 4),
            lax.rem(col + row // 2, 2),
            lax.rem(row, 2),
        ]
    ).astype(jnp.int32)
    where, iterate = lax.optimization_barrier((where, ks_matrix))
    half = iterate.astype(jnp.bfloat16)
    for _ in range(STEPS):
        iterate, half = newton_step(where, iterate, half, occupancy)
    return iterate


def solution(mesh):
    return jax.shard_map(
        body,
        mesh=mesh,
        in_specs=(P("row", "col"), P("row", "col")),
        out_specs=P("row", "col"),
        check_vma=False,
    )
```

```python
import functools
import itertools

import jax
import jax.numpy as jnp
from jax import lax
from jax.experimental import pallas as pl
from jax.experimental.pallas import tpu as pltpu
from jax.sharding import PartitionSpec as P

STEPS = 2
DIMS = (("y", 4), ("xh", 2), ("core", 2), ("z", 4), ("xl", 2))
OWN, BESIDE = (0, 0), (0, 1)
SLOTS = [(offset, pair) for offset in range(4) for pair in range(2)]
EARLY = (OWN, (3, 0), (1, 0), (2, 0), BESIDE)
LATE = ((3, 1), (1, 1), (2, 1))
LAST_LEFT = ((3, 1), (2, 1))
AT_HAND = tuple(at for at in SLOTS if at not in LAST_LEFT)


def pairs(move):
    sizes = [n for _, n in DIMS]
    names = [name for name, _ in DIMS]

    def flat(place):
        index = 0
        for name, n in DIMS:
            index = index * n + place[name] % n
        return index

    out = []
    for coords in itertools.product(*map(range, sizes)):
        place = dict(zip(names, coords))
        out.append((flat(place), flat({**place, **move(place)})))
    return out


Y_UP = pairs(lambda p: {"y": p["y"] + 1})
Y_DOWN = pairs(lambda p: {"y": p["y"] - 1})
Z_UP = pairs(lambda p: {"z": p["z"] + 1})
Z_DOWN = pairs(lambda p: {"z": p["z"] - 1})
INNER = pairs(lambda p: {"xl": 1 - p["xl"]})
OUTER = pairs(lambda p: {"xh": 1 - p["xh"], "xl": 1 - p["xl"]})
ACROSS = pairs(lambda p: {"xh": 1 - p["xh"]})
CORE = pairs(lambda p: {"core": 1 - p["core"]})

ANYWHERE = pl.BlockSpec(memory_space=pl.ANY)
VMEM = pl.BlockSpec(memory_space=pltpu.VMEM)
SMEM = pl.BlockSpec(memory_space=pltpu.SMEM)


def send(value, perm):
    return lax.ppermute(value, ("row", "col"), perm)


def join_send(values, perm):
    rows = values[0].shape[0]
    got = send(jnp.concatenate(values), perm)
    return [got[n * rows : (n + 1) * rows] for n in range(len(values))]


def settle(*values):
    return lax.optimization_barrier(values)


def call(kernel, operands, specs, shapes, out_specs, scratch, pieces, aliases=None):
    return pl.pallas_call(
        kernel,
        out_shape=shapes,
        in_specs=specs,
        out_specs=out_specs,
        scratch_shapes=scratch,
        input_output_aliases=aliases or {},
        compiler_params=pltpu.CompilerParams(vmem_limit_bytes=28 * 2**20),
        cost_estimate=pl.CostEstimate(
            flops=2 * 384 * 768 * 768 * pieces,
            bytes_accessed=3 * 2 * 384 * 768 * pieces,
            transcendentals=0,
        ),
    )(*operands)


def slot_of(where, at):
    offset, pair = at
    return 2 * lax.rem(offset - where[0] + 4, 4) + lax.rem(pair + where[1], 2)


def times(left, mine, other):
    right = jnp.concatenate([mine[...], other[...]], axis=0)
    return jnp.dot(left, right, preferred_element_type=jnp.float32)


def keep(where, at, mine, other, sorted_right, sem):
    core, lines = where[2], mine.shape[0]
    copies = []
    for n, (ref, half) in enumerate(((mine, core), (other, 1 - core))):
        start = pl.multiple_of(half * lines, lines)
        copy = pltpu.make_async_copy(
            ref, sorted_right.at[slot_of(where, at), pl.ds(start, lines)], sem.at[n]
        )
        copy.start()
        copies.append(copy)
    return copies


def swap_halves(where, source, target, sem):
    core, half = where[2], source.shape[1] // 2
    copies = []
    for part, at in enumerate((core, 1 - core)):
        start = pl.multiple_of(at * half, half)
        copies.append(
            pltpu.make_async_copy(
                source.at[:, pl.ds(start, half)],
                target.at[:, pl.ds(part * half, half)],
                sem.at[part],
            )
        )
    return copies


def lacking(slot):
    hits = [slot == SLOTS.index(at) for at in LAST_LEFT]
    return jnp.logical_or(*hits), hits[1].astype(jnp.int32)


def early_kernel(where, *refs):
    m, n = len(AT_HAND), len(EARLY)
    left, mine, other, refs = refs[:m], refs[m : m + n], refs[m + n : m + 2 * n], refs[m + 2 * n :]
    total, sorted_right, left_all, left_sem, keep_sem = refs
    copies, kept = [], []
    for k, at in enumerate(AT_HAND):
        copies += swap_halves(where, left[k], left_all.at[SLOTS.index(at)], left_sem.at[k])
    for copy in copies:
        copy.start()
    for k, at in enumerate(EARLY):
        kept += keep(where, at, mine[k], other[k], sorted_right, keep_sem.at[k])
    total[...] = jnp.zeros_like(total)
    for copy in copies:
        copy.wait()
    for k, at in enumerate(EARLY):
        slot = slot_of(where, at)

        @pl.when(jnp.logical_not(lacking(slot)[0]))
        def _(k=k, slot=slot):
            total[...] += times(left_all[slot], mine[k], other[k])

    for copy in kept:
        copy.wait()


def early(where, left, mine, other):
    rows, cols = left[OWN].shape
    m, n = len(AT_HAND), len(EARLY)
    return call(
        early_kernel,
        [where]
        + [left[at] for at in AT_HAND]
        + [mine[at] for at in EARLY]
        + [other[at] for at in EARLY],
        [SMEM] + [ANYWHERE] * m + [VMEM] * (2 * n),
        (
            jax.ShapeDtypeStruct((rows, cols), jnp.float32),
            jax.ShapeDtypeStruct((8, 2 * rows, cols), jnp.bfloat16),
        ),
        (VMEM, ANYWHERE),
        [
            pltpu.VMEM((8, rows, cols), jnp.bfloat16),
            pltpu.SemaphoreType.DMA((m, 2)),
            pltpu.SemaphoreType.DMA((n, 2)),
        ],
        n,
    )


def again_kernel(where, *refs):
    n, m = len(EARLY), len(LATE)
    left, mine, other, refs = refs[:8], refs[8 : 8 + n], refs[8 + n : 8 + 2 * n], refs[8 + 2 * n :]
    late, (old_total, total, picked) = refs[:m], refs[m:]
    half = picked.shape[2] // 2
    own = pl.ds(pl.multiple_of(where[2] * half, half), half)
    others = pl.ds(pl.multiple_of((1 - where[2]) * half, half), half)
    for k, at in enumerate(LATE):
        slot = slot_of(where, at)
        for n_left, ref in enumerate(left):

            @pl.when(slot == n_left)
            def _(k=k, ref=ref):
                picked[k, :, :half] = ref[:, own]
                picked[k, :, half:] = ref[:, others]

    value = old_total[...]
    for k, ref in enumerate(late):
        value += jnp.dot(picked[k, :, :half], ref[...], preferred_element_type=jnp.float32)
    total[...] = value
    for k, at in enumerate(EARLY):
        slot = slot_of(where, at)
        for last in LAST_LEFT:
            ref = left[SLOTS.index(last)]

            @pl.when(slot == SLOTS.index(last))
            def _(k=k, ref=ref):
                total[...] += jnp.dot(
                    ref[:, own], mine[k][...], preferred_element_type=jnp.float32
                ) + jnp.dot(ref[:, others], other[k][...], preferred_element_type=jnp.float32)


def again(where, left, mine, other, total):
    rows, cols = total.shape
    n, m = len(EARLY), len(LATE)
    return call(
        again_kernel,
        [where]
        + [left[at] for at in SLOTS]
        + [mine[at] for at in EARLY]
        + [other[at] for at in EARLY]
        + [mine[at] for at in LATE]
        + [total],
        [SMEM] + [VMEM] * (8 + 2 * n + m + 1),
        (
            jax.ShapeDtypeStruct((rows, cols), jnp.float32),
            jax.ShapeDtypeStruct((m, rows, cols), jnp.bfloat16),
        ),
        (VMEM, VMEM),
        [],
        3,
    )


def late_kernel(total, picked, *refs):
    other, square_half = refs[:-1], refs[-1]
    half = picked.shape[2] // 2
    value = total[...]
    for k, ref in enumerate(other):
        value += jnp.dot(picked[k, :, half:], ref[...], preferred_element_type=jnp.float32)
    square_half[...] = value.astype(jnp.bfloat16)


def late(total, picked, other):
    n = len(LATE)
    return call(
        late_kernel,
        [total, picked] + [other[at] for at in LATE],
        [VMEM] * (2 + n),
        jax.ShapeDtypeStruct(total.shape, jnp.bfloat16),
        VMEM,
        [],
        2,
    )


def place_kernel(where, *refs):
    n = len(LATE)
    mine, other, refs = refs[:n], refs[n : 2 * n], refs[2 * n :]
    _, sorted_right, keep_sem = refs
    kept = []
    for k, at in enumerate(LATE):
        kept += keep(where, at, mine[k], other[k], sorted_right, keep_sem.at[k])
    for copy in kept:
        copy.wait()


def place(where, mine, other, sorted_right):
    n = len(LATE)
    return call(
        place_kernel,
        [where] + [mine[at] for at in LATE] + [other[at] for at in LATE] + [sorted_right],
        [SMEM] + [ANYWHERE] * (2 * n + 1),
        jax.ShapeDtypeStruct(sorted_right.shape, sorted_right.dtype),
        ANYWHERE,
        [pltpu.SemaphoreType.DMA((n, 2))],
        2,
        {1 + 2 * n: 0},
    )


def product_kernel(ats, has_total, *refs):
    right, refs = refs[0], refs[1:]
    left, out = refs[-1 - len(ats) : -1], refs[-1]
    value = refs[0][...] if has_total else None
    for k, at in enumerate(ats):
        part = jnp.dot(
            left[k][...], right[SLOTS.index(at)], preferred_element_type=jnp.float32
        )
        value = part if value is None else value + part
    out[...] = value.astype(out.dtype)


def product(sorted_right, total, left, ats, dtype=jnp.float32):
    n = len(ats)
    has_total = total is not None
    return call(
        functools.partial(product_kernel, ats, has_total),
        [sorted_right] + ([total] if has_total else []) + [left[at] for at in ats],
        [VMEM] * (1 + n + has_total),
        jax.ShapeDtypeStruct(left[ats[0]].shape, dtype),
        VMEM,
        [],
        n,
    )


def final_kernel(at, occupancy, right, total, old, *refs):
    thirds, (new, new_half) = refs[:3], refs[3:]
    rows, cols = total.shape
    up, across = occupancy.shape
    block = rows // up
    left = jnp.concatenate([ref[...] for ref in thirds], axis=0)
    new[...] = total[...] + jnp.dot(
        left, right[SLOTS.index(at)], preferred_element_type=jnp.float32
    )
    for i in range(up):
        for j in range(across):
            here = (pl.ds(i * block, block), pl.ds(j * block, block))
            kept = occupancy[i, j].astype(jnp.float32)
            value = kept * (1.5 * old[here] - 0.5 * new[here])
            new[here] = value
            new_half[here] = value.astype(jnp.bfloat16)


def final(occupancy, sorted_right, total, old, thirds, at):
    rows, cols = total.shape
    return call(
        functools.partial(final_kernel, at),
        [occupancy, sorted_right, total, old, *thirds],
        [SMEM, VMEM, VMEM, VMEM] + [VMEM] * 3,
        (
            jax.ShapeDtypeStruct((rows, cols), jnp.float32),
            jax.ShapeDtypeStruct((rows, cols), jnp.bfloat16),
        ),
        (VMEM, VMEM),
        [],
        1,
    )


def newton_step(where, iterate, half, occupancy):
    middle = half.shape[0] // 2
    beside, z30, z10 = send(half, INNER), send(half, Z_UP), send(half, Z_DOWN)
    z10, z30, beside = settle(z10, z30, beside)
    y30, y10 = send(half, Y_UP), send(half, Y_DOWN)
    y10, y30, *_ = settle(y10, y30, z10, z30, beside)
    across, z11 = send(beside, OUTER), send(beside, Z_DOWN)
    z20 = send(z30, Z_UP)
    top, bottom = send(y30[:middle], Y_UP), send(y10[middle:], Y_DOWN)
    top, bottom, z11, z20, across, own = settle(top, bottom, z11, z20, across, half)
    y20 = jnp.concatenate([top, bottom])
    y31, y11, y21 = send(across, Y_UP), send(across, Y_DOWN), send(y20, ACROSS)
    *swapped, down = settle(*join_send((own, y30, y10, y20, across), CORE), z11)
    z31, z21 = send(beside, Z_UP), send(down, Z_DOWN)
    o = dict(zip(EARLY, swapped))
    y = {OWN: half, BESIDE: across, (3, 0): y30, (1, 0): y10, (2, 0): y20}
    z = {OWN: half, BESIDE: beside, (3, 0): z30, (1, 0): z10, (2, 0): z20, (1, 1): z11}
    total, sorted_right = early(where, z, y, o)
    total, sorted_right, y31, y11, y21, z31, z21 = settle(
        total, sorted_right, y31, y11, y21, z31, z21
    )
    z |= {(3, 1): z31, (2, 1): z21}
    y |= {(3, 1): y31, (1, 1): y11, (2, 1): y21}
    o |= dict(zip(LATE, join_send((y31, y11, y21), CORE)))
    total, picked = again(where, z, y, o, total)
    square_half = late(total, picked, o)
    square_half, sorted_right = settle(square_half, sorted_right)
    sorted_right = place(where, y, o, sorted_right)

    z = {OWN: square_half}
    z[1, 0], z[3, 0], z[BESIDE] = settle(
        send(square_half, Z_DOWN), send(square_half, Z_UP), send(square_half, INNER)
    )
    z20, z11, z31 = send(z[3, 0], Z_UP), send(z[BESIDE], Z_DOWN), send(z[3, 0], INNER)
    total = product(sorted_right, None, z, (OWN, (3, 0), (1, 0), BESIDE))
    z[2, 0], z[1, 1], z[3, 1] = z20, z11, z31
    low, high = half.shape[0] // 3, half.shape[0] * 3 // 4
    thirds = (
        send(z[3, 1][:low], Z_UP),
        send(z[1, 1][low:high], Z_DOWN),
        send(z[2, 0][high:], INNER),
    )
    total = product(sorted_right, total, z, ((2, 0), (1, 1), (3, 1)))
    return final(occupancy, sorted_right, total, iterate, thirds, (2, 1))


def body(ks_matrix, occupancy):
    row, col = lax.axis_index("row"), lax.axis_index("col")
    where = jnp.stack(
        [
            lax.rem(col // 2 - row // 4 + 4, 4),
            lax.rem(col + row // 2, 2),
            lax.rem(row, 2),
        ]
    ).astype(jnp.int32)
    where, iterate = lax.optimization_barrier((where, ks_matrix))
    half = iterate.astype(jnp.bfloat16)
    for _ in range(STEPS):
        iterate, half = newton_step(where, iterate, half, occupancy)
    return iterate


def solution(mesh):
    return jax.shard_map(
        body,
        mesh=mesh,
        in_specs=(P("row", "col"), P("row", "col")),
        out_specs=P("row", "col"),
        check_vma=False,
    )
```

```python
import functools
import itertools

import jax
import jax.numpy as jnp
from jax import lax
from jax.experimental import pallas as pl
from jax.experimental.pallas import tpu as pltpu
from jax.sharding import PartitionSpec as P

STEPS = 2
DIMS = (("y", 4), ("xh", 2), ("core", 2), ("z", 4), ("xl", 2))
OWN, BESIDE = (0, 0), (0, 1)
SLOTS = [(offset, pair) for offset in range(4) for pair in range(2)]
EARLY = (OWN, (3, 0), (1, 0), (2, 0), BESIDE)
LATE = ((3, 1), (1, 1), (2, 1))
LAST_LEFT = ((3, 1), (2, 1))
AT_HAND = tuple(at for at in SLOTS if at not in LAST_LEFT)


def pairs(move):
    sizes = [n for _, n in DIMS]
    names = [name for name, _ in DIMS]

    def flat(place):
        index = 0
        for name, n in DIMS:
            index = index * n + place[name] % n
        return index

    out = []
    for coords in itertools.product(*map(range, sizes)):
        place = dict(zip(names, coords))
        out.append((flat(place), flat({**place, **move(place)})))
    return out


Y_UP = pairs(lambda p: {"y": p["y"] + 1})
Y_DOWN = pairs(lambda p: {"y": p["y"] - 1})
Z_UP = pairs(lambda p: {"z": p["z"] + 1})
Z_DOWN = pairs(lambda p: {"z": p["z"] - 1})
INNER = pairs(lambda p: {"xl": 1 - p["xl"]})
OUTER = pairs(lambda p: {"xh": 1 - p["xh"], "xl": 1 - p["xl"]})
ACROSS = pairs(lambda p: {"xh": 1 - p["xh"]})
CORE = pairs(lambda p: {"core": 1 - p["core"]})

ANYWHERE = pl.BlockSpec(memory_space=pl.ANY)
VMEM = pl.BlockSpec(memory_space=pltpu.VMEM)
SMEM = pl.BlockSpec(memory_space=pltpu.SMEM)


def send(value, perm):
    return lax.ppermute(value, ("row", "col"), perm)


def join_send(values, perm):
    rows = values[0].shape[0]
    got = send(jnp.concatenate(values), perm)
    return [got[n * rows : (n + 1) * rows] for n in range(len(values))]


def settle(*values):
    return lax.optimization_barrier(values)


def call(kernel, operands, specs, shapes, out_specs, scratch, pieces, aliases=None):
    return pl.pallas_call(
        kernel,
        out_shape=shapes,
        in_specs=specs,
        out_specs=out_specs,
        scratch_shapes=scratch,
        input_output_aliases=aliases or {},
        compiler_params=pltpu.CompilerParams(vmem_limit_bytes=28 * 2**20),
        cost_estimate=pl.CostEstimate(
            flops=2 * 384 * 768 * 768 * pieces,
            bytes_accessed=3 * 2 * 384 * 768 * pieces,
            transcendentals=0,
        ),
    )(*operands)


def slot_of(where, at):
    offset, pair = at
    return 2 * lax.rem(offset - where[0] + 4, 4) + lax.rem(pair + where[1], 2)


def times(left, mine, other):
    right = jnp.concatenate([mine[...], other[...]], axis=0)
    return jnp.dot(left, right, preferred_element_type=jnp.float32)


def keep(where, at, mine, other, sorted_right, sem):
    core, lines = where[2], mine.shape[0]
    copies = []
    for n, (ref, half) in enumerate(((mine, core), (other, 1 - core))):
        start = pl.multiple_of(half * lines, lines)
        copy = pltpu.make_async_copy(
            ref, sorted_right.at[slot_of(where, at), pl.ds(start, lines)], sem.at[n]
        )
        copy.start()
        copies.append(copy)
    return copies


def swap_halves(where, source, target, sem):
    core, half = where[2], source.shape[1] // 2
    copies = []
    for part, at in enumerate((core, 1 - core)):
        start = pl.multiple_of(at * half, half)
        copies.append(
            pltpu.make_async_copy(
                source.at[:, pl.ds(start, half)],
                target.at[:, pl.ds(part * half, half)],
                sem.at[part],
            )
        )
    return copies


def lacking(slot):
    hits = [slot == SLOTS.index(at) for at in LAST_LEFT]
    return jnp.logical_or(*hits), hits[1].astype(jnp.int32)


def early_kernel(where, *refs):
    m, n = len(AT_HAND), len(EARLY)
    left, mine, other, refs = refs[:m], refs[m : m + n], refs[m + n : m + 2 * n], refs[m + 2 * n :]
    total, sorted_right, left_all, left_sem, keep_sem = refs
    copies, kept = [], []
    for k, at in enumerate(AT_HAND):
        copies += swap_halves(where, left[k], left_all.at[SLOTS.index(at)], left_sem.at[k])
    for copy in copies:
        copy.start()
    for k, at in enumerate(EARLY):
        kept += keep(where, at, mine[k], other[k], sorted_right, keep_sem.at[k])
    total[...] = jnp.zeros_like(total)
    for copy in copies:
        copy.wait()
    for k, at in enumerate(EARLY):
        slot = slot_of(where, at)

        @pl.when(jnp.logical_not(lacking(slot)[0]))
        def _(k=k, slot=slot):
            total[...] += times(left_all[slot], mine[k], other[k])

    for copy in kept:
        copy.wait()


def early(where, left, mine, other):
    rows, cols = left[OWN].shape
    m, n = len(AT_HAND), len(EARLY)
    return call(
        early_kernel,
        [where]
        + [left[at] for at in AT_HAND]
        + [mine[at] for at in EARLY]
        + [other[at] for at in EARLY],
        [SMEM] + [ANYWHERE] * m + [VMEM] * (2 * n),
        (
            jax.ShapeDtypeStruct((rows, cols), jnp.float32),
            jax.ShapeDtypeStruct((8, 2 * rows, cols), jnp.bfloat16),
        ),
        (VMEM, ANYWHERE),
        [
            pltpu.VMEM((8, rows, cols), jnp.bfloat16),
            pltpu.SemaphoreType.DMA((m, 2)),
            pltpu.SemaphoreType.DMA((n, 2)),
        ],
        n,
    )


def again_kernel(where, *refs):
    n, m = len(EARLY), len(LATE)
    left, mine, other, refs = refs[:8], refs[8 : 8 + n], refs[8 + n : 8 + 2 * n], refs[8 + 2 * n :]
    late, (old_total, total, picked) = refs[:m], refs[m:]
    half = picked.shape[2] // 2
    own = pl.ds(pl.multiple_of(where[2] * half, half), half)
    others = pl.ds(pl.multiple_of((1 - where[2]) * half, half), half)
    for k, at in enumerate(LATE):
        slot = slot_of(where, at)
        for n_left, ref in enumerate(left):

            @pl.when(slot == n_left)
            def _(k=k, ref=ref):
                picked[k, :, :half] = ref[:, own]
                picked[k, :, half:] = ref[:, others]

    value = old_total[...]
    for k, ref in enumerate(late):
        value += jnp.dot(picked[k, :, :half], ref[...], preferred_element_type=jnp.float32)
    total[...] = value
    for k, at in enumerate(EARLY):
        slot = slot_of(where, at)
        for last in LAST_LEFT:
            ref = left[SLOTS.index(last)]

            @pl.when(slot == SLOTS.index(last))
            def _(k=k, ref=ref):
                total[...] += jnp.dot(
                    ref[:, own], mine[k][...], preferred_element_type=jnp.float32
                ) + jnp.dot(ref[:, others], other[k][...], preferred_element_type=jnp.float32)


def again(where, left, mine, other, total):
    rows, cols = total.shape
    n, m = len(EARLY), len(LATE)
    return call(
        again_kernel,
        [where]
        + [left[at] for at in SLOTS]
        + [mine[at] for at in EARLY]
        + [other[at] for at in EARLY]
        + [mine[at] for at in LATE]
        + [total],
        [SMEM] + [VMEM] * (8 + 2 * n + m + 1),
        (
            jax.ShapeDtypeStruct((rows, cols), jnp.float32),
            jax.ShapeDtypeStruct((m, rows, cols), jnp.bfloat16),
        ),
        (VMEM, VMEM),
        [],
        3,
    )


def late_kernel(total, picked, *refs):
    other, square_half = refs[:-1], refs[-1]
    half = picked.shape[2] // 2
    value = total[...]
    for k, ref in enumerate(other):
        value += jnp.dot(picked[k, :, half:], ref[...], preferred_element_type=jnp.float32)
    square_half[...] = value.astype(jnp.bfloat16)


def late(total, picked, other):
    n = len(LATE)
    return call(
        late_kernel,
        [total, picked] + [other[at] for at in LATE],
        [VMEM] * (2 + n),
        jax.ShapeDtypeStruct(total.shape, jnp.bfloat16),
        VMEM,
        [],
        2,
    )


def place_kernel(where, *refs):
    n = len(LATE)
    mine, other, refs = refs[:n], refs[n : 2 * n], refs[2 * n :]
    _, sorted_right, keep_sem = refs
    kept = []
    for k, at in enumerate(LATE):
        kept += keep(where, at, mine[k], other[k], sorted_right, keep_sem.at[k])
    for copy in kept:
        copy.wait()


def place(where, mine, other, sorted_right):
    n = len(LATE)
    return call(
        place_kernel,
        [where] + [mine[at] for at in LATE] + [other[at] for at in LATE] + [sorted_right],
        [SMEM] + [ANYWHERE] * (2 * n + 1),
        jax.ShapeDtypeStruct(sorted_right.shape, sorted_right.dtype),
        ANYWHERE,
        [pltpu.SemaphoreType.DMA((n, 2))],
        2,
        {1 + 2 * n: 0},
    )


def product_kernel(ats, has_total, *refs):
    right, refs = refs[0], refs[1:]
    left, out = refs[-1 - len(ats) : -1], refs[-1]
    value = refs[0][...] if has_total else None
    for k, at in enumerate(ats):
        part = jnp.dot(
            left[k][...], right[SLOTS.index(at)], preferred_element_type=jnp.float32
        )
        value = part if value is None else value + part
    out[...] = value.astype(out.dtype)


def product(sorted_right, total, left, ats, dtype=jnp.float32):
    n = len(ats)
    has_total = total is not None
    return call(
        functools.partial(product_kernel, ats, has_total),
        [sorted_right] + ([total] if has_total else []) + [left[at] for at in ats],
        [VMEM] * (1 + n + has_total),
        jax.ShapeDtypeStruct(left[ats[0]].shape, dtype),
        VMEM,
        [],
        n,
    )


def final_kernel(at, occupancy, right, total, old, *refs):
    thirds, (new, new_half) = refs[:3], refs[3:]
    rows, cols = total.shape
    up, across = occupancy.shape
    block = rows // up
    left = jnp.concatenate([ref[...] for ref in thirds], axis=0)
    new[...] = total[...] + jnp.dot(
        left, right[SLOTS.index(at)], preferred_element_type=jnp.float32
    )
    for i in range(up):
        for j in range(across):
            here = (pl.ds(i * block, block), pl.ds(j * block, block))
            kept = occupancy[i, j].astype(jnp.float32)
            value = kept * (1.5 * old[here] - 0.5 * new[here])
            new[here] = value
            new_half[here] = value.astype(jnp.bfloat16)


def final(occupancy, sorted_right, total, old, thirds, at):
    rows, cols = total.shape
    return call(
        functools.partial(final_kernel, at),
        [occupancy, sorted_right, total, old, *thirds],
        [SMEM, VMEM, VMEM, VMEM] + [VMEM] * 3,
        (
            jax.ShapeDtypeStruct((rows, cols), jnp.float32),
            jax.ShapeDtypeStruct((rows, cols), jnp.bfloat16),
        ),
        (VMEM, VMEM),
        [],
        1,
    )


def newton_step(where, iterate, half, occupancy):
    middle = half.shape[0] // 2
    beside, z30, z10 = send(half, INNER), send(half, Z_UP), send(half, Z_DOWN)
    z10, z30, beside = settle(z10, z30, beside)
    y30, y10 = send(half, Y_UP), send(half, Y_DOWN)
    y10, y30, *_ = settle(y10, y30, z10, z30, beside)
    across, z11 = send(beside, OUTER), send(beside, Z_DOWN)
    z20 = send(z30, Z_UP)
    top, bottom = send(y30[:middle], Y_UP), send(y10[middle:], Y_DOWN)
    top, bottom, z11, z20, across, own = settle(top, bottom, z11, z20, across, half)
    y20 = jnp.concatenate([top, bottom])
    y31, y11, y21 = send(across, Y_UP), send(across, Y_DOWN), send(y20, ACROSS)
    *swapped, down = settle(*join_send((own, y30, y10, y20, across), CORE), z11)
    z31, z21 = send(beside, Z_UP), send(down, Z_DOWN)
    o = dict(zip(EARLY, swapped))
    y = {OWN: half, BESIDE: across, (3, 0): y30, (1, 0): y10, (2, 0): y20}
    z = {OWN: half, BESIDE: beside, (3, 0): z30, (1, 0): z10, (2, 0): z20, (1, 1): z11}
    total, sorted_right = early(where, z, y, o)
    total, sorted_right, y31, y11, y21, z31, z21 = settle(
        total, sorted_right, y31, y11, y21, z31, z21
    )
    z |= {(3, 1): z31, (2, 1): z21}
    y |= {(3, 1): y31, (1, 1): y11, (2, 1): y21}
    o |= dict(zip(LATE, join_send((y31, y11, y21), CORE)))
    total, picked = again(where, z, y, o, total)
    square_half = late(total, picked, o)
    square_half, sorted_right = settle(square_half, sorted_right)
    sorted_right = place(where, y, o, sorted_right)

    z = {OWN: square_half}
    z[1, 0], z[3, 0], z[BESIDE] = settle(
        send(square_half, Z_DOWN), send(square_half, Z_UP), send(square_half, INNER)
    )
    z20, z11, z31 = send(z[3, 0], Z_UP), send(z[BESIDE], Z_DOWN), send(z[3, 0], INNER)
    total = product(sorted_right, None, z, (OWN, (3, 0), (1, 0), BESIDE))
    z[2, 0], z[1, 1], z[3, 1] = z20, z11, z31
    low, high = half.shape[0] // 4, half.shape[0] * 17 // 24
    thirds = (
        send(z[3, 1][:low], Z_UP),
        send(z[1, 1][low:high], Z_DOWN),
        send(z[2, 0][high:], INNER),
    )
    total = product(sorted_right, total, z, ((2, 0), (1, 1), (3, 1)))
    return final(occupancy, sorted_right, total, iterate, thirds, (2, 1))


def body(ks_matrix, occupancy):
    row, col = lax.axis_index("row"), lax.axis_index("col")
    where = jnp.stack(
        [
            lax.rem(col // 2 - row // 4 + 4, 4),
            lax.rem(col + row // 2, 2),
            lax.rem(row, 2),
        ]
    ).astype(jnp.int32)
    where, iterate = lax.optimization_barrier((where, ks_matrix))
    half = iterate.astype(jnp.bfloat16)
    for _ in range(STEPS):
        iterate, half = newton_step(where, iterate, half, occupancy)
    return iterate


def solution(mesh):
    return jax.shard_map(
        body,
        mesh=mesh,
        in_specs=(P("row", "col"), P("row", "col")),
        out_specs=P("row", "col"),
        check_vma=False,
    )
```

```python
import functools
import itertools

import jax
import jax.numpy as jnp
from jax import lax
from jax.experimental import pallas as pl
from jax.experimental.pallas import tpu as pltpu
from jax.sharding import PartitionSpec as P

STEPS = 2
DIMS = (("y", 4), ("xh", 2), ("core", 2), ("z", 4), ("xl", 2))
OWN, BESIDE = (0, 0), (0, 1)
SLOTS = [(offset, pair) for offset in range(4) for pair in range(2)]
EARLY = (OWN, (3, 0), (1, 0), (2, 0), BESIDE)
LATE = ((3, 1), (1, 1), (2, 1))
LAST_LEFT = ((3, 1), (2, 1))
AT_HAND = tuple(at for at in SLOTS if at not in LAST_LEFT)


def pairs(move):
    sizes = [n for _, n in DIMS]
    names = [name for name, _ in DIMS]

    def flat(place):
        index = 0
        for name, n in DIMS:
            index = index * n + place[name] % n
        return index

    out = []
    for coords in itertools.product(*map(range, sizes)):
        place = dict(zip(names, coords))
        out.append((flat(place), flat({**place, **move(place)})))
    return out


Y_UP = pairs(lambda p: {"y": p["y"] + 1})
Y_DOWN = pairs(lambda p: {"y": p["y"] - 1})
Z_UP = pairs(lambda p: {"z": p["z"] + 1})
Z_DOWN = pairs(lambda p: {"z": p["z"] - 1})
INNER = pairs(lambda p: {"xl": 1 - p["xl"]})
OUTER = pairs(lambda p: {"xh": 1 - p["xh"], "xl": 1 - p["xl"]})
ACROSS = pairs(lambda p: {"xh": 1 - p["xh"]})
CORE = pairs(lambda p: {"core": 1 - p["core"]})

ANYWHERE = pl.BlockSpec(memory_space=pl.ANY)
VMEM = pl.BlockSpec(memory_space=pltpu.VMEM)
SMEM = pl.BlockSpec(memory_space=pltpu.SMEM)


def send(value, perm):
    return lax.ppermute(value, ("row", "col"), perm)


def join_send(values, perm):
    rows = values[0].shape[0]
    got = send(jnp.concatenate(values), perm)
    return [got[n * rows : (n + 1) * rows] for n in range(len(values))]


def settle(*values):
    return lax.optimization_barrier(values)


def call(kernel, operands, specs, shapes, out_specs, scratch, pieces, aliases=None):
    return pl.pallas_call(
        kernel,
        out_shape=shapes,
        in_specs=specs,
        out_specs=out_specs,
        scratch_shapes=scratch,
        input_output_aliases=aliases or {},
        compiler_params=pltpu.CompilerParams(vmem_limit_bytes=28 * 2**20),
        cost_estimate=pl.CostEstimate(
            flops=2 * 384 * 768 * 768 * pieces,
            bytes_accessed=3 * 2 * 384 * 768 * pieces,
            transcendentals=0,
        ),
    )(*operands)


def slot_of(where, at):
    offset, pair = at
    return 2 * lax.rem(offset - where[0] + 4, 4) + lax.rem(pair + where[1], 2)


def times(left, mine, other):
    right = jnp.concatenate([mine[...], other[...]], axis=0)
    return jnp.dot(left, right, preferred_element_type=jnp.float32)


def keep(where, at, mine, other, sorted_right, sem):
    core, lines = where[2], mine.shape[0]
    copies = []
    for n, (ref, half) in enumerate(((mine, core), (other, 1 - core))):
        start = pl.multiple_of(half * lines, lines)
        copy = pltpu.make_async_copy(
            ref, sorted_right.at[slot_of(where, at), pl.ds(start, lines)], sem.at[n]
        )
        copy.start()
        copies.append(copy)
    return copies


def swap_halves(where, source, target, sem):
    core, half = where[2], source.shape[1] // 2
    copies = []
    for part, at in enumerate((core, 1 - core)):
        start = pl.multiple_of(at * half, half)
        copies.append(
            pltpu.make_async_copy(
                source.at[:, pl.ds(start, half)],
                target.at[:, pl.ds(part * half, half)],
                sem.at[part],
            )
        )
    return copies


def lacking(slot):
    hits = [slot == SLOTS.index(at) for at in LAST_LEFT]
    return jnp.logical_or(*hits), hits[1].astype(jnp.int32)


def early_kernel(where, *refs):
    m, n = len(AT_HAND), len(EARLY)
    left, mine, other, refs = refs[:m], refs[m : m + n], refs[m + n : m + 2 * n], refs[m + 2 * n :]
    total, sorted_right, left_all, left_sem, keep_sem = refs
    copies, kept = [], []
    for k, at in enumerate(AT_HAND):
        copies += swap_halves(where, left[k], left_all.at[SLOTS.index(at)], left_sem.at[k])
    for copy in copies:
        copy.start()
    for k, at in enumerate(EARLY):
        kept += keep(where, at, mine[k], other[k], sorted_right, keep_sem.at[k])
    total[...] = jnp.zeros_like(total)
    for copy in copies:
        copy.wait()
    for k, at in enumerate(EARLY):
        slot = slot_of(where, at)

        @pl.when(jnp.logical_not(lacking(slot)[0]))
        def _(k=k, slot=slot):
            total[...] += times(left_all[slot], mine[k], other[k])

    for copy in kept:
        copy.wait()


def early(where, left, mine, other):
    rows, cols = left[OWN].shape
    m, n = len(AT_HAND), len(EARLY)
    return call(
        early_kernel,
        [where]
        + [left[at] for at in AT_HAND]
        + [mine[at] for at in EARLY]
        + [other[at] for at in EARLY],
        [SMEM] + [ANYWHERE] * m + [VMEM] * (2 * n),
        (
            jax.ShapeDtypeStruct((rows, cols), jnp.float32),
            jax.ShapeDtypeStruct((8, 2 * rows, cols), jnp.bfloat16),
        ),
        (VMEM, ANYWHERE),
        [
            pltpu.VMEM((8, rows, cols), jnp.bfloat16),
            pltpu.SemaphoreType.DMA((m, 2)),
            pltpu.SemaphoreType.DMA((n, 2)),
        ],
        n,
    )


def again_kernel(where, *refs):
    n, m = len(EARLY), len(LATE)
    left, mine, other, refs = refs[:8], refs[8 : 8 + n], refs[8 + n : 8 + 2 * n], refs[8 + 2 * n :]
    late, (old_total, total, picked) = refs[:m], refs[m:]
    half = picked.shape[2] // 2
    own = pl.ds(pl.multiple_of(where[2] * half, half), half)
    others = pl.ds(pl.multiple_of((1 - where[2]) * half, half), half)
    for k, at in enumerate(LATE):
        slot = slot_of(where, at)
        for n_left, ref in enumerate(left):

            @pl.when(slot == n_left)
            def _(k=k, ref=ref):
                picked[k, :, :half] = ref[:, own]
                picked[k, :, half:] = ref[:, others]

    value = old_total[...]
    for k, ref in enumerate(late):
        value += jnp.dot(picked[k, :, :half], ref[...], preferred_element_type=jnp.float32)
    total[...] = value
    for k, at in enumerate(EARLY):
        slot = slot_of(where, at)
        for last in LAST_LEFT:
            ref = left[SLOTS.index(last)]

            @pl.when(slot == SLOTS.index(last))
            def _(k=k, ref=ref):
                total[...] += jnp.dot(
                    ref[:, own], mine[k][...], preferred_element_type=jnp.float32
                ) + jnp.dot(ref[:, others], other[k][...], preferred_element_type=jnp.float32)


def again(where, left, mine, other, total):
    rows, cols = total.shape
    n, m = len(EARLY), len(LATE)
    return call(
        again_kernel,
        [where]
        + [left[at] for at in SLOTS]
        + [mine[at] for at in EARLY]
        + [other[at] for at in EARLY]
        + [mine[at] for at in LATE]
        + [total],
        [SMEM] + [VMEM] * (8 + 2 * n + m + 1),
        (
            jax.ShapeDtypeStruct((rows, cols), jnp.float32),
            jax.ShapeDtypeStruct((m, rows, cols), jnp.bfloat16),
        ),
        (VMEM, VMEM),
        [],
        3,
    )


def late_kernel(total, picked, *refs):
    other, square_half = refs[:-1], refs[-1]
    half = picked.shape[2] // 2
    value = total[...]
    for k, ref in enumerate(other):
        value += jnp.dot(picked[k, :, half:], ref[...], preferred_element_type=jnp.float32)
    square_half[...] = value.astype(jnp.bfloat16)


def late(total, picked, other):
    n = len(LATE)
    return call(
        late_kernel,
        [total, picked] + [other[at] for at in LATE],
        [VMEM] * (2 + n),
        jax.ShapeDtypeStruct(total.shape, jnp.bfloat16),
        VMEM,
        [],
        2,
    )


def place_kernel(where, *refs):
    n = len(LATE)
    mine, other, refs = refs[:n], refs[n : 2 * n], refs[2 * n :]
    _, sorted_right, keep_sem = refs
    kept = []
    for k, at in enumerate(LATE):
        kept += keep(where, at, mine[k], other[k], sorted_right, keep_sem.at[k])
    for copy in kept:
        copy.wait()


def place(where, mine, other, sorted_right):
    n = len(LATE)
    return call(
        place_kernel,
        [where] + [mine[at] for at in LATE] + [other[at] for at in LATE] + [sorted_right],
        [SMEM] + [ANYWHERE] * (2 * n + 1),
        jax.ShapeDtypeStruct(sorted_right.shape, sorted_right.dtype),
        ANYWHERE,
        [pltpu.SemaphoreType.DMA((n, 2))],
        2,
        {1 + 2 * n: 0},
    )


def product_kernel(ats, has_total, *refs):
    right, refs = refs[0], refs[1:]
    left, out = refs[-1 - len(ats) : -1], refs[-1]
    value = refs[0][...] if has_total else None
    for k, at in enumerate(ats):
        part = jnp.dot(
            left[k][...], right[SLOTS.index(at)], preferred_element_type=jnp.float32
        )
        value = part if value is None else value + part
    out[...] = value.astype(out.dtype)


def product(sorted_right, total, left, ats, dtype=jnp.float32):
    n = len(ats)
    has_total = total is not None
    return call(
        functools.partial(product_kernel, ats, has_total),
        [sorted_right] + ([total] if has_total else []) + [left[at] for at in ats],
        [VMEM] * (1 + n + has_total),
        jax.ShapeDtypeStruct(left[ats[0]].shape, dtype),
        VMEM,
        [],
        n,
    )


def final_kernel(at, occupancy, right, total, old, *refs):
    thirds, (new, new_half) = refs[:3], refs[3:]
    rows, cols = total.shape
    up, across = occupancy.shape
    block = rows // up
    left = jnp.concatenate([ref[...] for ref in thirds], axis=0)
    new[...] = total[...] + jnp.dot(
        left, right[SLOTS.index(at)], preferred_element_type=jnp.float32
    )
    for i in range(up):
        for j in range(across):
            here = (pl.ds(i * block, block), pl.ds(j * block, block))
            kept = occupancy[i, j].astype(jnp.float32)
            value = kept * (1.5 * old[here] - 0.5 * new[here])
            new[here] = value
            new_half[here] = value.astype(jnp.bfloat16)


def final(occupancy, sorted_right, total, old, thirds, at):
    rows, cols = total.shape
    return call(
        functools.partial(final_kernel, at),
        [occupancy, sorted_right, total, old, *thirds],
        [SMEM, VMEM, VMEM, VMEM] + [VMEM] * 3,
        (
            jax.ShapeDtypeStruct((rows, cols), jnp.float32),
            jax.ShapeDtypeStruct((rows, cols), jnp.bfloat16),
        ),
        (VMEM, VMEM),
        [],
        1,
    )


def newton_step(where, iterate, half, occupancy):
    middle = half.shape[0] // 2
    beside, z30, z10 = send(half, INNER), send(half, Z_UP), send(half, Z_DOWN)
    z10, z30, beside = settle(z10, z30, beside)
    y30, y10 = send(half, Y_UP), send(half, Y_DOWN)
    y10, y30, *_ = settle(y10, y30, z10, z30, beside)
    across, z11 = send(beside, OUTER), send(beside, Z_DOWN)
    z20 = send(z30, Z_UP)
    top, bottom = send(y30[:middle], Y_UP), send(y10[middle:], Y_DOWN)
    top, bottom, z11, z20, across, own = settle(top, bottom, z11, z20, across, half)
    y20 = jnp.concatenate([top, bottom])
    y31, y11, y21 = send(across, Y_UP), send(across, Y_DOWN), send(y20, ACROSS)
    *swapped, down = settle(*join_send((own, y30, y10, y20, across), CORE), z11)
    z31, z21 = send(beside, Z_UP), send(down, Z_DOWN)
    o = dict(zip(EARLY, swapped))
    y = {OWN: half, BESIDE: across, (3, 0): y30, (1, 0): y10, (2, 0): y20}
    z = {OWN: half, BESIDE: beside, (3, 0): z30, (1, 0): z10, (2, 0): z20, (1, 1): z11}
    total, sorted_right = early(where, z, y, o)
    total, sorted_right, y31, y11, y21, z31, z21 = settle(
        total, sorted_right, y31, y11, y21, z31, z21
    )
    z |= {(3, 1): z31, (2, 1): z21}
    y |= {(3, 1): y31, (1, 1): y11, (2, 1): y21}
    o |= {at: send(y[at], CORE) for at in LATE}
    total, picked = again(where, z, y, o, total)
    square_half = late(total, picked, o)
    square_half, sorted_right = settle(square_half, sorted_right)
    sorted_right = place(where, y, o, sorted_right)

    z = {OWN: square_half}
    z[1, 0], z[3, 0], z[BESIDE] = settle(
        send(square_half, Z_DOWN), send(square_half, Z_UP), send(square_half, INNER)
    )
    z20, z11, z31 = send(z[3, 0], Z_UP), send(z[BESIDE], Z_DOWN), send(z[3, 0], INNER)
    total = product(sorted_right, None, z, (OWN, (3, 0), (1, 0), BESIDE))
    z[2, 0], z[1, 1], z[3, 1] = z20, z11, z31
    low, high = half.shape[0] // 4, half.shape[0] * 17 // 24
    thirds = (
        send(z[3, 1][:low], Z_UP),
        send(z[1, 1][low:high], Z_DOWN),
        send(z[2, 0][high:], INNER),
    )
    total = product(sorted_right, total, z, ((2, 0), (1, 1), (3, 1)))
    return final(occupancy, sorted_right, total, iterate, thirds, (2, 1))


def body(ks_matrix, occupancy):
    row, col = lax.axis_index("row"), lax.axis_index("col")
    where = jnp.stack(
        [
            lax.rem(col // 2 - row // 4 + 4, 4),
            lax.rem(col + row // 2, 2),
            lax.rem(row, 2),
        ]
    ).astype(jnp.int32)
    where, iterate = lax.optimization_barrier((where, ks_matrix))
    half = iterate.astype(jnp.bfloat16)
    for _ in range(STEPS):
        iterate, half = newton_step(where, iterate, half, occupancy)
    return iterate


def solution(mesh):
    return jax.shard_map(
        body,
        mesh=mesh,
        in_specs=(P("row", "col"), P("row", "col")),
        out_specs=P("row", "col"),
        check_vma=False,
    )
```
